256 devices in a mesh: grp: 8 (over x, y_hi), intra: 32 (over y_lo, z, core).
Axes of the slice: x: 4, y: 4 (y_hi: 2, y_lo: 2; y = y_hi * 2 + y_lo), z: 8, core: 2. Of those that a mesh axis runs over, the one named last changes fastest.
Arguments:
- tokens: bfloat16 [65536, 8192], P(('grp', 'intra')), may hold values from -24 to 24
- cotangent: bfloat16 [65536, 512], P(('grp', 'intra')), may hold values from -6 to 6
- next_tokens: bfloat16 [65536, 8192], P(('grp', 'intra')), may hold values from -6 to 6
- master: float32 [8192, 512], P(('grp', 'intra')), may hold values from -0.0625 to 0.0625
- moment_one: float32 [8192, 512], P(('grp', 'intra')), may hold values from -0.012 to 0.012
- moment_two: float32 [8192, 512], P(('grp', 'intra')), may hold values from 1e-06 to 0.0001
Outputs:
- new_master: float32 [8192, 512], P(('grp', 'intra'))
- new_moment_one: float32 [8192, 512], P(('grp', 'intra'))
- new_moment_two: float32 [8192, 512], P(('grp', 'intra'))
- next_out: bfloat16 [65536, 512], P(('grp', 'intra'))
The draws below stay inside these ranges and needn't reach their ends.
All inputs are finite; a program needn't handle non-finite values.
Results may differ from the reference program's by a relative error of at most 0.0049.
Values may be sent and summed in bfloat16 or wider, within the bound.
No kernel may reach another device: no remote copies, remote signals or barrier semaphores. Data moves between devices by JAX's collectives and lax.ppermute only.
A program may use at most 128 MiB of HBM per device.

```python
import math
import jax
import jax.numpy as jnp

D = 8192
FB = 512
TOKENS = 65536


def strengthened(drawn, stream_key, source, target, parts, factor):
    def block_of(position):
        return (jnp.arange(drawn.shape[position]) // (drawn.shape[position] // parts)).reshape((-1,) + (1,) * (drawn.ndim - 1 - position))

    first = jax.random.permutation(stream_key, parts)[block_of(target)]
    far = (block_of(target) + parts // 2) % parts
    return jnp.where((block_of(source) == first) | (block_of(source) == far), factor * drawn, drawn)


def block_scale(key, dims, split, low, top_value):
    gain, own = 1.0, jax.random.fold_in(key, 6)
    for axis_at, shards_of in split:
        draws = jnp.exp(jax.random.uniform(jax.random.fold_in(own, axis_at), (shards_of,), jnp.float32, low / len(split), top_value / len(split)))
        gain = gain * jnp.repeat(draws, dims[axis_at] // shards_of).reshape([-1 if axis == axis_at else 1 for axis in range(len(dims))])
    return gain


def noise(rng, shape, width, bound, pieces=(), dtype=jnp.bfloat16):
    drawn = width * jax.random.normal(rng, shape, jnp.float32)
    if pieces:
        drawn = drawn * block_scale(rng, shape, pieces, -0.22, 0.18)
    return jnp.clip(drawn, -bound, bound).astype(dtype)


def bell_draw_with(own_key, shape, width, bound, pieces, heavy, held_as=jnp.bfloat16):
    entries = width * jax.random.normal(own_key, shape, jnp.float32)
    if pieces:
        entries = entries * block_scale(own_key, shape, pieces, -0.22, 0.18)
    return jnp.clip(strengthened(entries, jax.random.fold_in(own_key, 3), *heavy), -bound, bound).astype(held_as)


def setup_inputs(seed: int = 0) -> dict:
    arg_keys = jax.random.split(jax.random.key(seed), 7)
    return {
        "tokens": bell_draw_with(arg_keys[0], (TOKENS, D), 1.0, 24.0, ((0, 256),), (0, 1, 256, 6.0)),
        "cotangent": noise(arg_keys[1], (TOKENS, FB), 1.0, 6.0, ((0, 256),)),
        "next_tokens": noise(arg_keys[2], (TOKENS, D), 1.0, 6.0, ((0, 256),)),
        "master": noise(arg_keys[3], (D, FB), D ** -0.5, 0.0625, ((0, 256),), jnp.float32),
        "moment_one": noise(arg_keys[4], (D, FB), 0.002, 0.012, ((0, 256),), jnp.float32),
        "moment_two": jnp.clip(jnp.exp(math.log(0.0001) - 4.6051702 * jax.random.uniform(arg_keys[5], (D, FB), jnp.float32) ** block_scale(arg_keys[5], (D, FB), ((0, 256),), -0.2, 0.2)), 9.999999974752427e-07, 0.0001),
    }


def reference(tokens, cotangent, next_tokens, master, moment_one, moment_two):
    gradient = jnp.dot(tokens.T, cotangent, preferred_element_type=jnp.float32) * (1.0 / TOKENS)
    new_moment_one = 0.9 * moment_one + 0.1 * gradient
    new_moment_two = 0.999 * moment_two + 0.001 * gradient * gradient
    first = new_moment_one / (1.0 - 0.9 ** 10)
    second = new_moment_two / (1.0 - 0.999 ** 10)
    new_master = master - 0.01 * (first / (jnp.sqrt(second) + 1e-08) + 0.1 * master)
    weights = new_master.astype(jnp.bfloat16)
    next_out = jnp.dot(next_tokens, weights, preferred_element_type=jnp.float32).astype(jnp.bfloat16)
    return (new_master, new_moment_one, new_moment_two, next_out)
```

```python
import functools

import jax
import jax.numpy as jnp
from jax import lax
from jax.experimental import pallas as pl
from jax.experimental.pallas import tpu as pltpu
from jax.sharding import PartitionSpec as P

AXES = ("grp", "intra")
DEVICES = 256
VMEM_LIMIT = 48 * 1024 * 1024


def coordinates(d):
    return d // 64, d // 16 % 4, d // 2 % 8, d % 2


def flat(x, y, z, c):
    return (x % 4) * 64 + (y % 4) * 16 + (z % 8) * 2 + c


def near(z, c):
    return z ^ 1 if c == 0 else ((z + 1) % 8 if z % 2 else (z - 1) % 8)


def far(z, c):
    return near(z // 2, c) % 4 * 2 + z % 2 if c == 0 or z // 2 % 2 else (z // 2 - 1) % 4 * 2 + z % 2


def neighbour(d, da, dz, wide):
    x, y, z, c = coordinates(d)
    if dz:
        z = near(z, c) if wide else far(z, c)
    if (c == 0) == wide:
        x = x + da
    else:
        y = y + da
    return flat(x, y, z, c)


def groups(wide):
    seen = {}
    for d in range(DEVICES):
        members = []
        for parity in range(2):
            _, _, z, _ = coordinates(d)
            here = (z if wide else z // 2) % 2
            for a in range(4):
                x, y, z, c = coordinates(neighbour(d, 0, int(here != parity), wide))
                members.append(flat(a, y, z, c) if (c == 0) == wide else flat(x, a, z, c))
        seen[tuple(members)] = None
    return [list(members) for members in seen]


def home(d, flip):
    x, y, z, c = coordinates(d)
    return flat(x % 2 + 2 * c, y, z ^ (4 * flip), x // 2)


def permute(value, target):
    return lax.ppermute(value, AXES, [(d, target(d)) for d in range(DEVICES)])


OFFSETS = [(1, 0), (3, 0), (0, 1), (2, 0), (1, 1), (3, 1), (2, 1)]


def block_at(c, j, g):
    x_lo, y = j // 4, j % 4
    z2, z1, z0, k = g // 8, g // 4 % 2, g // 2 % 2, g % 2
    first, second = 2 * k + x_lo, y
    a = jnp.where(c == 0, first, second)
    b = jnp.where(c == 0, second, first)
    return z0 * 64 + a * 16 + z1 * 8 + b * 2 + z2


def gradient_kernel(rows, core_ref, mine_ref, theirs_ref, my_cot_ref, their_cot_ref, out_ref):
    c, j = core_ref[0], pl.program_id(0)
    dims = (((0,), (0,)), ((), ()))
    total = lax.dot_general(mine_ref[...], my_cot_ref[...], dims, preferred_element_type=jnp.float32)
    total += lax.dot_general(theirs_ref[...], their_cot_ref[...], dims, preferred_element_type=jnp.float32)
    total = total.astype(out_ref.dtype)
    for g in range(total.shape[0] // rows):
        out_ref[block_at(c, j, g)] = total[g * rows : (g + 1) * rows]


def gradient_blocks(core, tokens, theirs, my_cot, their_cot, rows):
    t, f = my_cot.shape
    half = theirs.shape[1]
    wide = 16 * rows
    steps = half // wide
    return pl.pallas_call(
        functools.partial(gradient_kernel, rows),
        grid_spec=pltpu.PrefetchScalarGridSpec(
            num_scalar_prefetch=1,
            grid=(steps,),
            in_specs=[
                pl.BlockSpec((t, wide), lambda j, core: (0, core[0] * steps + j)),
                pl.BlockSpec((t, wide), lambda j, core: (0, j)),
                pl.BlockSpec((t, f), lambda j, core: (0, 0)),
                pl.BlockSpec((t, f), lambda j, core: (0, 0)),
            ],
            out_specs=pl.BlockSpec((half // rows, rows, f), lambda j, core: (0, 0, 0)),
        ),
        out_shape=jax.ShapeDtypeStruct((half // rows, rows, f), jnp.bfloat16),
        compiler_params=pltpu.CompilerParams(vmem_limit_bytes=VMEM_LIMIT),
        cost_estimate=pl.CostEstimate(
            flops=4 * t * half * f, bytes_accessed=4 * t * half + 2 * half * f, transcendentals=0
        ),
        name="gradient_blocks",
    )(core, tokens, theirs, my_cot, their_cot)


def place_kernel(where_ref, *refs):
    out_ref = refs[-1]
    for i, ref in enumerate(refs[:-1]):
        out_ref[where_ref[i]] = ref[...]


def place(where, pieces):
    n = len(pieces)
    return pl.pallas_call(
        place_kernel,
        in_specs=[pl.BlockSpec(memory_space=pltpu.SMEM)] + [pl.BlockSpec(memory_space=pltpu.VMEM)] * n,
        out_specs=pl.BlockSpec(memory_space=pltpu.VMEM),
        out_shape=jax.ShapeDtypeStruct((n,) + pieces[0].shape, pieces[0].dtype),
        name="place",
    )(where, *pieces)


def forward_kernel(rows, n, at_ref, mine_ref, theirs_ref, *refs):
    pieces, (my_out, their_out, weights, total, sems) = refs[:n], refs[n:]
    c, j = at_ref[n], pl.program_id(0)
    t = mine_ref.shape[0]

    @pl.when(j == 0)
    def _():
        copies = [
            pltpu.make_async_copy(piece, weights.at[at_ref[i]], sems.at[i]) for i, piece in enumerate(pieces)
        ]
        for copy in copies:
            copy.start()
        total[...] = jnp.zeros_like(total)
        for copy in copies:
            copy.wait()

    blocks = []
    for g in range(mine_ref.shape[1] // rows):
        at = block_at(c, j, g)
        blocks.append(weights[at // 16, at % 16])
    chunk = jnp.concatenate(blocks, axis=0)
    total[:t] += jnp.dot(mine_ref[...], chunk, preferred_element_type=jnp.float32)
    total[t:] += jnp.dot(theirs_ref[...], chunk, preferred_element_type=jnp.float32)

    @pl.when(j == pl.num_programs(0) - 1)
    def _():
        my_out[...] = total[:t]
        their_out[...] = total[t:].astype(their_out.dtype)


def forward(at, tokens, theirs, pieces, rows):
    t, half = theirs.shape
    n, per, _, f = (len(pieces),) + pieces[0].shape
    wide = 16 * rows
    steps = half // wide
    return pl.pallas_call(
        functools.partial(forward_kernel, rows, n),
        grid_spec=pltpu.PrefetchScalarGridSpec(
            num_scalar_prefetch=1,
            grid=(steps,),
            in_specs=[
                pl.BlockSpec((t, wide), lambda j, at: (0, at[n] * steps + j)),
                pl.BlockSpec((t, wide), lambda j, at: (0, j)),
            ]
            + [pl.BlockSpec(memory_space=pl.ANY)] * n,
            out_specs=[pl.BlockSpec((t, f), lambda j, at: (0, 0))] * 2,
            scratch_shapes=[
                pltpu.VMEM((n, per, rows, f), jnp.bfloat16),
                pltpu.VMEM((2 * t, f), jnp.float32),
                pltpu.SemaphoreType.DMA((n,)),
            ],
        ),
        out_shape=[
            jax.ShapeDtypeStruct((t, f), jnp.float32),
            jax.ShapeDtypeStruct((t, f), jnp.bfloat16),
        ],
        compiler_params=pltpu.CompilerParams(vmem_limit_bytes=VMEM_LIMIT),
        cost_estimate=pl.CostEstimate(
            flops=4 * t * half * f, bytes_accessed=4 * t * half + 2 * half * f, transcendentals=0
        ),
        name="forward",
    )(at, tokens, theirs, *pieces)


def summed(stacked):
    return stacked.astype(jnp.float32).sum(axis=0)


def on_device(tokens, cotangent, next_tokens, master, moment_one, moment_two):
    rows, f = master.shape
    t, d = tokens.shape
    half = d // 2
    me = lax.axis_index("grp") * 32 + lax.axis_index("intra")
    x, y, z, c = coordinates(me)
    other_core = lambda v: permute(v, lambda d: d ^ 1)

    def other_half(v):
        return jnp.where(c == 0, v[:, half:], v[:, :half])

    theirs = other_core(other_half(tokens))
    their_cot = other_core(cotangent)
    core = jnp.reshape(c, (1,)).astype(jnp.int32)

    partial = gradient_blocks(core, tokens, theirs, cotangent, their_cot, rows)
    partial = partial.reshape(8, 16, rows, f)
    partial = lax.all_to_all(partial, AXES, 0, 0, tiled=True, axis_index_groups=groups(True))
    partial = summed(partial).astype(jnp.bfloat16).reshape(8, 2, rows, f)
    partial = lax.all_to_all(partial, AXES, 0, 0, tiled=True, axis_index_groups=groups(False))
    partial = summed(partial)
    z2 = z // 4
    same = jnp.where(z2 == 0, partial[0], partial[1]).astype(jnp.bfloat16)
    twin = jnp.where(z2 == 0, partial[1], partial[0]).astype(jnp.bfloat16)
    same = permute(same, lambda d: home(d, 0))
    twin = permute(twin, lambda d: home(d, 1))
    total = same.astype(jnp.float32) + twin.astype(jnp.float32)

    gradient = total * (1.0 / (t * DEVICES))
    new_moment_one = 0.9 * moment_one + 0.1 * gradient
    new_moment_two = 0.999 * moment_two + 0.001 * gradient * gradient
    first = new_moment_one / (1.0 - 0.9**10)
    second = new_moment_two / (1.0 - 0.999**10)
    new_master = master - 0.01 * (first / (jnp.sqrt(second) + 1e-08) + 0.1 * master)
    weights = new_master.astype(jnp.bfloat16)

    next_theirs = other_core(other_half(next_tokens))
    same = permute(weights, lambda d: home(d, 0))
    twin = permute(weights, lambda d: home(d, 1))
    two = jnp.where(z2 == 0, jnp.stack([same, twin]), jnp.stack([twin, same]))
    offsets = OFFSETS + [(0, 0)]

    def places(a, parity):
        return [(parity ^ dz) * 4 + (a - da) % 4 for da, dz in offsets]

    a, b = jnp.where(c == 0, x, y), jnp.where(c == 0, y, x)
    pieces = [permute(two, lambda d: neighbour(d, da, dz, False)) for da, dz in OFFSETS] + [two]
    where = jnp.stack(places(b, z // 2 % 2)).astype(jnp.int32)
    sixteen = place(where, pieces).reshape(16, rows, f)
    pieces = [permute(sixteen, lambda d: neighbour(d, da, dz, True)) for da, dz in OFFSETS] + [sixteen]
    at = jnp.stack(places(a, z % 2) + [c]).astype(jnp.int32)
    my_out, their_out = forward(at, next_tokens, next_theirs, pieces, rows)
    result = my_out + other_core(their_out).astype(jnp.float32)
    return (new_master, new_moment_one, new_moment_two, result.astype(jnp.bfloat16))


def solution(mesh):
    spec = P(AXES, None)
    return jax.shard_map(on_device, mesh=mesh, in_specs=(spec,) * 6, out_specs=(spec,) * 4, check_vma=False)
```

```python
import functools

import jax
import jax.numpy as jnp
from jax import lax
from jax.experimental import pallas as pl
from jax.experimental.pallas import tpu as pltpu
from jax.sharding import PartitionSpec as P

AXES = ("grp", "intra")
DEVICES = 256
SIZES = (4, 4, 8)
ORDER = ((0, 1, 2), (1, 2, 0), (2, 0, 1))
LANES = 128
VMEM_LIMIT = 24 * 1024 * 1024
FIRST_LIMIT = 48 * 1024 * 1024


def coordinates(d):
    return d // 64, d // 16 % 4, d // 2 % 8, d % 2


def flat(x, y, z, c):
    return x * 64 + y * 16 + z * 2 + c


def neighbour(d, axis):
    at, c = list(coordinates(d)[:3]), d % 2
    at[axis] = (at[axis] + (1 if at[axis] % 2 == c else -1)) % SIZES[axis]
    return flat(*at, c)


def permute(value, target):
    return lax.ppermute(value, AXES, [(d, target(d)) for d in range(DEVICES)])


def groups():
    seen = {}
    for d in range(DEVICES):
        x, y, z, c = coordinates(d)
        seen.setdefault((x % 2, y % 2, z % 2, c), []).append(d)
    return list(seen.values())


def part_rows(f):
    tiles = f // 16
    first = (tiles + 2) // 3 * 16
    return (first, first, f - 2 * first)


def place_in(part, rel, x1, y1):
    a, b, c = (rel[axis] for axis in ORDER[part])
    return a, (b * 2 + c) * 4 + x1 * 2 + y1


def sort_kernel(at_ref, in_ref, my_ref, other_ref, chunks, sems):
    c, x0, y0, z0 = (at_ref[i] for i in range(4))
    wide = chunks.shape[2]
    copies = []
    for i in range(4):
        start = pl.multiple_of((2 * (i % 2) + (x0 ^ (i // 2))) * wide, wide)
        copies.append(pltpu.make_async_copy(in_ref.at[:, pl.ds(start, wide)], chunks.at[i], sems.at[i]))
        copies[-1].start()
    n = 4 * LANES
    source = lax.broadcasted_iota(jnp.int32, (n, n), 0)
    goal = lax.broadcasted_iota(jnp.int32, (n, n), 1)
    q, r, row = goal // 128, goal // 32 % 4, goal % 32
    wanted = r * 128 + (((q % 2) ^ z0) * 2 + ((q // 2) ^ c)) * 32 + row
    move = jnp.where(source == wanted, 1.0, 0.0).astype(my_ref.dtype)
    for i in range(4):
        copies[i].wait()
        for y in range(4):
            turned = jnp.dot(chunks[i, :, y * n : (y + 1) * n], move, preferred_element_type=jnp.float32)
            turned = turned.astype(my_ref.dtype)
            where = (y0 ^ (y % 2)) * 4 + (y // 2) * 2
            for rz in range(2):
                my_ref[i, where + rz] = turned[:, rz * LANES : (rz + 1) * LANES]
                other_ref[i, where + rz] = turned[:, (2 + rz) * LANES : (3 + rz) * LANES]


def sort_columns(at, tokens, limit):
    t, d = tokens.shape
    space = pl.BlockSpec(memory_space=pltpu.VMEM)
    return pl.pallas_call(
        sort_kernel,
        in_specs=[pl.BlockSpec(memory_space=pltpu.SMEM), pl.BlockSpec(memory_space=pl.ANY)],
        out_specs=[space, space],
        out_shape=[jax.ShapeDtypeStruct((4, 8, t, LANES), tokens.dtype)] * 2,
        scratch_shapes=[pltpu.VMEM((4, t, d // 4), tokens.dtype), pltpu.SemaphoreType.DMA((4,))],
        compiler_params=pltpu.CompilerParams(vmem_limit_bytes=limit),
        cost_estimate=pl.CostEstimate(flops=8 * LANES * t * d, bytes_accessed=4 * t * d, transcendentals=0),
        name="sort_columns",
    )(at, tokens)


def gradient_kernel(parts, mine_ref, theirs_ref, my_cot_ref, their_cot_ref, *out_refs):
    cot = jnp.concatenate([my_cot_ref[...].T, their_cot_ref[...].T], axis=1)
    starts = [sum(parts[:p]) for p in range(3)]
    for rx in range(2):
        for x1 in range(2):
            for ry in range(2):
                blocks = [
                    jnp.concatenate([mine_ref[rx * 2 + x1, ry * 4 + i], theirs_ref[rx * 2 + x1, ry * 4 + i]], axis=0)
                    for i in range(4)
                ]
                total = jnp.dot(cot, jnp.concatenate(blocks, axis=1), preferred_element_type=jnp.float32)
                total = total.astype(jnp.bfloat16)
                for y1 in range(2):
                    for rz in range(2):
                        i = y1 * 2 + rz
                        for p in range(3):
                            half, at = place_in(p, (rx, ry, rz), x1, y1)
                            out_refs[2 * p + half][:, at * LANES : (at + 1) * LANES] = total[
                                starts[p] : starts[p] + parts[p], i * LANES : (i + 1) * LANES
                            ]


def vmem_call(kernel, outs, name, flops, *operands):
    size = sum(a.size * a.dtype.itemsize for a in operands) + sum(o.size * o.dtype.itemsize for o in outs)
    space = pl.BlockSpec(memory_space=pltpu.VMEM)
    return pl.pallas_call(
        kernel,
        in_specs=[space] * len(operands),
        out_specs=[space] * len(outs),
        out_shape=outs,
        compiler_params=pltpu.CompilerParams(vmem_limit_bytes=VMEM_LIMIT),
        cost_estimate=pl.CostEstimate(flops=flops, bytes_accessed=size, transcendentals=0),
        name=name,
    )(*operands)


def rows_kernel(*refs):
    kept, came, out_ref = refs[0:6:2], refs[1:6:2], refs[6]
    sums = [k[...].astype(jnp.float32) + r[...].astype(jnp.float32) for k, r in zip(kept, came)]
    out_ref[...] = jnp.concatenate(sums, axis=0).T.astype(out_ref.dtype)


def columns_kernel(parts, in_ref, *out_refs):
    turned = in_ref[...].astype(jnp.float32).T.astype(in_ref.dtype)
    for p, out in enumerate(out_refs):
        start = sum(parts[:p])
        out[...] = turned[start : start + parts[p]]


def half_product(part, half, token_refs, weight_ref):
    tokens = [None] * 16
    for rx in range(2):
        for ry in range(2):
            for rz in range(2):
                for x1 in range(2):
                    for y1 in range(2):
                        side, at = place_in(part, (rx, ry, rz), x1, y1)
                        if side == half:
                            block = [ref[rx * 2 + x1, ry * 4 + y1 * 2 + rz] for ref in token_refs]
                            tokens[at] = jnp.concatenate(block, axis=0)
    return lax.dot_general(
        jnp.concatenate(tokens, axis=1), weight_ref[...], (((1,), (1,)), ((), ())), preferred_element_type=jnp.float32
    )


def forward_own_kernel(mine_ref, theirs_ref, *refs):
    for p in range(3):
        refs[3 + p][...] = half_product(p, 0, (mine_ref, theirs_ref), refs[p])


def forward_kernel(first, tokens_ref, *refs):
    t = tokens_ref.shape[2]
    weights, before, out_ref = refs[:3], refs[3:6], refs[6]
    total = [before[p][first : first + t] + half_product(p, 1, (tokens_ref,), weights[p]) for p in range(3)]
    out_ref[...] = jnp.concatenate(total, axis=1).astype(out_ref.dtype)


def update_kernel(scale, partial_ref, master_ref, one_ref, two_ref, new_master, new_one, new_two, copies):
    gradient = partial_ref[...].astype(jnp.float32).sum(axis=0) * scale
    one = 0.9 * one_ref[...] + 0.1 * gradient
    two = 0.999 * two_ref[...] + 0.001 * gradient * gradient
    first = one / (1.0 - 0.9**10)
    second = two / (1.0 - 0.999**10)
    master = master_ref[...]
    master = master - 0.01 * (first / (jnp.sqrt(second) + 1e-08) + 0.1 * master)
    new_one[...] = one
    new_two[...] = two
    new_master[...] = master
    copies[...] = jnp.broadcast_to(master.astype(copies.dtype)[None], copies.shape)


def halved(value):
    n = value.shape[1] // 2
    return value[:, :n], value[:, n:]


def on_device(tokens, cotangent, next_tokens, master, moment_one, moment_two):
    rows, f = master.shape
    t, d = tokens.shape
    half = d // 2
    parts = part_rows(f)
    me = lax.axis_index("grp") * 32 + lax.axis_index("intra")
    x, y, z, c = coordinates(me)
    at = jnp.stack([c, x % 2, y % 2, z % 2]).astype(jnp.int32)
    bf16 = lambda *shape: jax.ShapeDtypeStruct(shape, jnp.bfloat16)
    f32 = lambda *shape: jax.ShapeDtypeStruct(shape, jnp.float32)
    other_core = lambda v: permute(v, lambda d: d ^ 1)
    flops = 4 * t * half * f

    their_cot = other_core(cotangent)
    mine, sent = sort_columns(at, tokens, FIRST_LIMIT)
    theirs = other_core(sent)
    halves = vmem_call(
        functools.partial(gradient_kernel, parts),
        [bf16(p, half // 2) for p in parts for _ in range(2)],
        "gradient",
        flops,
        mine,
        theirs,
        cotangent,
        their_cot,
    )
    last = []
    for p in range(3):
        kept, sent = halves[2 * p : 2 * p + 2]
        for i, axis in enumerate(ORDER[p]):
            came = permute(sent.astype(jnp.bfloat16), lambda d: neighbour(d, axis))
            if i < 2:
                kept, sent = halved(kept.astype(jnp.float32) + came.astype(jnp.float32))
        last += [kept, came]
    (partial,) = vmem_call(rows_kernel, [bf16(16 * rows, f)], "rows", 0, *last)
    partial = partial.reshape(16, rows, f)
    partial = lax.all_to_all(partial, AXES, 0, 0, tiled=True, axis_index_groups=groups())
    new_master, new_moment_one, new_moment_two, copies = vmem_call(
        functools.partial(update_kernel, 1.0 / (t * DEVICES)),
        [f32(rows, f)] * 3 + [bf16(16, rows, f)],
        "update",
        0,
        partial,
        master,
        moment_one,
        moment_two,
    )

    next_mine, next_sent = sort_columns(at, next_tokens, VMEM_LIMIT)
    next_theirs = other_core(next_sent)
    copies = lax.all_to_all(copies, AXES, 0, 0, tiled=True, axis_index_groups=groups())
    held = vmem_call(
        functools.partial(columns_kernel, parts),
        [bf16(p, 16 * rows) for p in parts],
        "columns",
        0,
        copies.reshape(16 * rows, f),
    )
    owns, cames = [], []
    for p in range(3):
        own = held[p]
        for i, axis in enumerate(ORDER[p][::-1]):
            came = permute(own, lambda d: neighbour(d, axis))
            if i < 2:
                own = jnp.concatenate([own, came], axis=1)
        owns.append(own)
        cames.append(came)
    before = vmem_call(
        forward_own_kernel, [f32(2 * t, p) for p in parts], "forward_own", flops // 2, next_mine, next_theirs, *owns
    )
    (their_out,) = vmem_call(
        functools.partial(forward_kernel, t), [bf16(t, f)], "forward_theirs", flops // 4, next_theirs, *cames, *before
    )
    their_out = other_core(their_out)
    (my_out,) = vmem_call(
        functools.partial(forward_kernel, 0), [f32(t, f)], "forward_mine", flops // 4, next_mine, *cames, *before
    )
    result = my_out + their_out.astype(jnp.float32)
    return (new_master, new_moment_one, new_moment_two, result.astype(jnp.bfloat16))


def solution(mesh):
    spec = P(AXES, None)
    return jax.shard_map(on_device, mesh=mesh, in_specs=(spec,) * 6, out_specs=(spec,) * 4, check_vma=False)
```

```python
import functools

import jax
import jax.numpy as jnp
from jax import lax
from jax.experimental import pallas as pl
from jax.experimental.pallas import tpu as pltpu
from jax.sharding import PartitionSpec as P

AXES = ("grp", "intra")
DEVICES = 256
SIZES = (4, 4, 8)
ORDER = ((0, 1, 2), (1, 2, 0), (2, 0, 1))
LANES = 128
VMEM_LIMIT = 24 * 1024 * 1024
FIRST_LIMIT = 48 * 1024 * 1024


def coordinates(d):
    return d // 64, d // 16 % 4, d // 2 % 8, d % 2


def flat(x, y, z, c):
    return x * 64 + y * 16 + z * 2 + c


def neighbour(d, axis):
    at, c = list(coordinates(d)[:3]), d % 2
    at[axis] = (at[axis] + (1 if at[axis] % 2 == c else -1)) % SIZES[axis]
    return flat(*at, c)


def permute(value, target):
    return lax.ppermute(value, AXES, [(d, target(d)) for d in range(DEVICES)])


def groups():
    seen = {}
    for d in range(DEVICES):
        x, y, z, c = coordinates(d)
        seen.setdefault((x % 2, y % 2, z % 2, c), []).append(d)
    return list(seen.values())


def part_rows(f):
    tiles = f // 16
    first = (tiles + 2) // 3 * 16
    return (first, first, f - 2 * first)


def place_in(part, rel, x1, y1):
    a, b, c = (rel[axis] for axis in ORDER[part])
    return a, (b * 2 + c) * 4 + x1 * 2 + y1


def sort_kernel(sides, at_ref, in_ref, my_ref, other_ref, chunks, sems):
    c, x0, y0, z0 = (at_ref[i] for i in range(4))
    wide = chunks.shape[2]
    copies = []
    for i in range(2 * len(sides)):
        start = pl.multiple_of((2 * (i % 2) + (x0 ^ sides[i // 2])) * wide, wide)
        copies.append(pltpu.make_async_copy(in_ref.at[:, pl.ds(start, wide)], chunks.at[i], sems.at[i]))
        copies[-1].start()
    n = 4 * LANES
    source = lax.broadcasted_iota(jnp.int32, (n, n), 0)
    goal = lax.broadcasted_iota(jnp.int32, (n, n), 1)
    q, r, row = goal // 128, goal // 32 % 4, goal % 32
    wanted = r * 128 + (((q % 2) ^ z0) * 2 + ((q // 2) ^ c)) * 32 + row
    move = jnp.where(source == wanted, 1.0, 0.0).astype(my_ref.dtype)
    for i in range(2 * len(sides)):
        copies[i].wait()
        for y in range(4):
            turned = jnp.dot(chunks[i, :, y * n : (y + 1) * n], move, preferred_element_type=jnp.float32)
            turned = turned.astype(my_ref.dtype)
            where = (y0 ^ (y % 2)) * 4 + (y // 2) * 2
            for rz in range(2):
                my_ref[i, where + rz] = turned[:, rz * LANES : (rz + 1) * LANES]
                other_ref[i, where + rz] = turned[:, (2 + rz) * LANES : (3 + rz) * LANES]


def sort_columns(at, tokens, sides, limit):
    t, d = tokens.shape
    n = 2 * len(sides)
    space = pl.BlockSpec(memory_space=pltpu.VMEM)
    return pl.pallas_call(
        functools.partial(sort_kernel, sides),
        in_specs=[pl.BlockSpec(memory_space=pltpu.SMEM), pl.BlockSpec(memory_space=pl.ANY)],
        out_specs=[space, space],
        out_shape=[jax.ShapeDtypeStruct((n, 8, t, LANES), tokens.dtype)] * 2,
        scratch_shapes=[pltpu.VMEM((n, t, d // 4), tokens.dtype), pltpu.SemaphoreType.DMA((n,))],
        compiler_params=pltpu.CompilerParams(vmem_limit_bytes=limit),
        cost_estimate=pl.CostEstimate(
            flops=2 * n * LANES * t * d, bytes_accessed=n * t * d, transcendentals=0
        ),
        name="sort_columns",
    )(at, tokens)


def gradient_blocks(mine_ref, theirs_ref, my_cot_ref, their_cot_ref):
    cot = jnp.concatenate([my_cot_ref[...].T, their_cot_ref[...].T], axis=1)
    for x1 in range(2):
        for ry in range(2):
            blocks = [
                jnp.concatenate([mine_ref[x1, ry * 4 + i], theirs_ref[x1, ry * 4 + i]], axis=0) for i in range(4)
            ]
            total = jnp.dot(cot, jnp.concatenate(blocks, axis=1), preferred_element_type=jnp.float32)
            yield x1, ry, total.astype(jnp.bfloat16)


def lanes(at):
    return slice(at * LANES, (at + 1) * LANES)


def gradient_far_kernel(parts, mine_ref, theirs_ref, my_cot_ref, their_cot_ref, sent_ref, *held_refs):
    starts = [sum(parts[:p]) for p in range(3)]
    for x1, ry, total in gradient_blocks(mine_ref, theirs_ref, my_cot_ref, their_cot_ref):
        for i in range(4):
            y1, rz = i // 2, i % 2
            _, at = place_in(0, (1, ry, rz), x1, y1)
            sent_ref[:, lanes(at)] = total[: parts[0], lanes(i)]
        for p in (1, 2):
            at = (ry * 2 + x1) * 4 * LANES
            held_refs[p - 1][:, at : at + 4 * LANES] = total[starts[p] : starts[p] + parts[p]]


def gradient_near_kernel(parts, mine_ref, theirs_ref, my_cot_ref, their_cot_ref, *refs):
    held_refs, out_refs = (None,) + refs[:2], refs[2:]
    starts = [sum(parts[:p]) for p in range(3)]
    for x1, ry, total in gradient_blocks(mine_ref, theirs_ref, my_cot_ref, their_cot_ref):
        for i in range(4):
            y1, rz = i // 2, i % 2
            for p in range(3):
                half, at = place_in(p, (0, ry, rz), x1, y1)
                out = out_refs[2 * p + half - (p > 0)]
                out[:, lanes(at)] = total[starts[p] : starts[p] + parts[p], lanes(i)]
                if p:
                    half, at = place_in(p, (1, ry, rz), x1, y1)
                    out = out_refs[2 * p + half - 1]
                    out[:, lanes(at)] = held_refs[p][:, lanes((ry * 2 + x1) * 4 + i)]


def vmem_call(kernel, outs, name, flops, *operands):
    size = sum(a.size * a.dtype.itemsize for a in operands) + sum(o.size * o.dtype.itemsize for o in outs)
    space = pl.BlockSpec(memory_space=pltpu.VMEM)
    return pl.pallas_call(
        kernel,
        in_specs=[space] * len(operands),
        out_specs=[space] * len(outs),
        out_shape=outs,
        compiler_params=pltpu.CompilerParams(vmem_limit_bytes=VMEM_LIMIT),
        cost_estimate=pl.CostEstimate(flops=flops, bytes_accessed=size, transcendentals=0),
        name=name,
    )(*operands)


def rows_kernel(*refs):
    kept, came, out_ref = refs[0:6:2], refs[1:6:2], refs[6]
    sums = [k[...].astype(jnp.float32) + r[...].astype(jnp.float32) for k, r in zip(kept, came)]
    out_ref[...] = jnp.concatenate(sums, axis=0).T.astype(out_ref.dtype)


def columns_kernel(parts, in_ref, *out_refs):
    turned = in_ref[...].astype(jnp.float32).T.astype(in_ref.dtype)
    for p, out in enumerate(out_refs):
        start = sum(parts[:p])
        out[...] = turned[start : start + parts[p]]


def half_product(part, half, token_refs, weight_ref):
    tokens = [None] * 16
    for rx in range(2):
        for ry in range(2):
            for rz in range(2):
                for x1 in range(2):
                    for y1 in range(2):
                        side, at = place_in(part, (rx, ry, rz), x1, y1)
                        if side == half:
                            block = [ref[rx * 2 + x1, ry * 4 + y1 * 2 + rz] for ref in token_refs]
                            tokens[at] = jnp.concatenate(block, axis=0)
    return lax.dot_general(
        jnp.concatenate(tokens, axis=1), weight_ref[...], (((1,), (1,)), ((), ())), preferred_element_type=jnp.float32
    )


def forward_own_kernel(mine_ref, theirs_ref, *refs):
    for p in range(3):
        refs[3 + p][...] = half_product(p, 0, (mine_ref, theirs_ref), refs[p])
    refs[6][...] = theirs_ref[...]


def forward_kernel(first, tokens_ref, *refs):
    t = tokens_ref.shape[2]
    weights, before, out_ref = refs[:3], refs[3:6], refs[6]
    total = [before[p][first : first + t] + half_product(p, 1, (tokens_ref,), weights[p]) for p in range(3)]
    out_ref[...] = jnp.concatenate(total, axis=1).astype(out_ref.dtype)


def update_kernel(scale, partial_ref, master_ref, one_ref, two_ref, new_master, new_one, new_two, copies):
    gradient = partial_ref[...].astype(jnp.float32).sum(axis=0) * scale
    one = 0.9 * one_ref[...] + 0.1 * gradient
    two = 0.999 * two_ref[...] + 0.001 * gradient * gradient
    first = one / (1.0 - 0.9**10)
    second = two / (1.0 - 0.999**10)
    master = master_ref[...]
    master = master - 0.01 * (first / (jnp.sqrt(second) + 1e-08) + 0.1 * master)
    new_one[...] = one
    new_two[...] = two
    new_master[...] = master
    copies[...] = jnp.broadcast_to(master.astype(copies.dtype)[None], copies.shape)


def halved(value):
    n = value.shape[1] // 2
    return value[:, :n], value[:, n:]


def on_device(tokens, cotangent, next_tokens, master, moment_one, moment_two):
    rows, f = master.shape
    t, d = tokens.shape
    half = d // 2
    parts = part_rows(f)
    me = lax.axis_index("grp") * 32 + lax.axis_index("intra")
    x, y, z, c = coordinates(me)
    at = jnp.stack([c, x % 2, y % 2, z % 2]).astype(jnp.int32)
    bf16 = lambda *shape: jax.ShapeDtypeStruct(shape, jnp.bfloat16)
    f32 = lambda *shape: jax.ShapeDtypeStruct(shape, jnp.float32)
    other_core = lambda v: permute(v, lambda d: d ^ 1)
    flops = 4 * t * half * f

    their_cot = other_core(cotangent)
    mine_far, sent = sort_columns(at, tokens, (1,), FIRST_LIMIT)
    theirs_far = other_core(sent)
    mine_near, sent = sort_columns(at, tokens, (0,), FIRST_LIMIT)
    theirs_near = other_core(sent)
    sent_0, *held = vmem_call(
        functools.partial(gradient_far_kernel, parts),
        [bf16(p, half // 2) for p in parts],
        "gradient_far",
        flops // 2,
        mine_far,
        theirs_far,
        cotangent,
        their_cot,
    )
    kept_0, *halves = vmem_call(
        functools.partial(gradient_near_kernel, parts),
        [bf16(parts[0], half // 2)] + [bf16(p, half // 2) for p in parts[1:] for _ in range(2)],
        "gradient_near",
        flops // 2,
        mine_near,
        theirs_near,
        cotangent,
        their_cot,
        *held,
    )
    halves = [kept_0, sent_0] + halves
    last = []
    for p in range(3):
        kept, sent = halves[2 * p : 2 * p + 2]
        for i, axis in enumerate(ORDER[p]):
            came = permute(sent.astype(jnp.bfloat16), lambda d: neighbour(d, axis))
            if i < 2:
                kept, sent = halved(kept.astype(jnp.float32) + came.astype(jnp.float32))
        last += [kept, came]
    (partial,) = vmem_call(rows_kernel, [bf16(16 * rows, f)], "rows", 0, *last)
    partial = partial.reshape(16, rows, f)
    partial = lax.all_to_all(partial, AXES, 0, 0, tiled=True, axis_index_groups=groups())
    new_master, new_moment_one, new_moment_two, copies = vmem_call(
        functools.partial(update_kernel, 1.0 / (t * DEVICES)),
        [f32(rows, f)] * 3 + [bf16(16, rows, f)],
        "update",
        0,
        partial,
        master,
        moment_one,
        moment_two,
    )

    next_mine, next_sent = sort_columns(at, next_tokens, (0, 1), VMEM_LIMIT)
    next_theirs = other_core(next_sent)
    copies = lax.all_to_all(copies, AXES, 0, 0, tiled=True, axis_index_groups=groups())
    held = vmem_call(
        functools.partial(columns_kernel, parts),
        [bf16(p, 16 * rows) for p in parts],
        "columns",
        0,
        copies.reshape(16 * rows, f),
    )
    owns, cames = [], []
    for p in range(3):
        own = held[p]
        for i, axis in enumerate(ORDER[p][::-1]):
            came = permute(own, lambda d: neighbour(d, axis))
            if i < 2:
                own = jnp.concatenate([own, came], axis=1)
        owns.append(own)
        cames.append(came)
    *before, next_theirs = vmem_call(
        forward_own_kernel,
        [f32(2 * t, p) for p in parts] + [bf16(*next_theirs.shape)],
        "forward_own",
        flops // 2,
        next_mine,
        next_theirs,
        *owns,
    )
    (their_out,) = vmem_call(
        functools.partial(forward_kernel, t), [bf16(t, f)], "forward_theirs", flops // 4, next_theirs, *cames, *before
    )
    their_out = other_core(their_out)
    (my_out,) = vmem_call(
        functools.partial(forward_kernel, 0), [f32(t, f)], "forward_mine", flops // 4, next_mine, *cames, *before
    )
    result = my_out + their_out.astype(jnp.float32)
    return (new_master, new_moment_one, new_moment_two, result.astype(jnp.bfloat16))


def solution(mesh):
    spec = P(AXES, None)
    return jax.shard_map(on_device, mesh=mesh, in_specs=(spec,) * 6, out_specs=(spec,) * 4, check_vma=False)
```

```python
import functools

import jax
import jax.numpy as jnp
from jax import lax
from jax.experimental import pallas as pl
from jax.experimental.pallas import tpu as pltpu
from jax.sharding import PartitionSpec as P

AXES = ("grp", "intra")
DEVICES = 256
SIZES = (4, 4, 8)
ORDER = ((0, 1, 2), (1, 2, 0), (2, 0, 1))
LANES = 128
VMEM_LIMIT = 24 * 1024 * 1024
FIRST_LIMIT = 48 * 1024 * 1024


def coordinates(d):
    return d // 64, d // 16 % 4, d // 2 % 8, d % 2


def flat(x, y, z, c):
    return x * 64 + y * 16 + z * 2 + c


def neighbour(d, axis):
    at, c = list(coordinates(d)[:3]), d % 2
    at[axis] = (at[axis] + (1 if at[axis] % 2 == c else -1)) % SIZES[axis]
    return flat(*at, c)


def permute(value, target):
    return lax.ppermute(value, AXES, [(d, target(d)) for d in range(DEVICES)])


def twin(d):
    x, y, z, c = coordinates(d)
    return flat(x, y, z ^ 4, c)


def groups():
    seen = {}
    for d in range(DEVICES):
        x, y, z, c = coordinates(d)
        seen.setdefault((x % 2, y % 2, z % 2, z // 4, c), []).append(d)
    return list(seen.values())


def part_rows(f):
    tiles = f // 16
    first = (tiles + 2) // 3 * 16
    return (first, first, f - 2 * first)


def place_in(part, rel, x1, y1):
    a, b, c = (rel[axis] for axis in ORDER[part])
    return a, (b * 2 + c) * 4 + x1 * 2 + y1


def sort_kernel(at_ref, in_ref, my_ref, other_ref, chunks, sems):
    c, x0, y0, z0 = (at_ref[i] for i in range(4))
    wide = chunks.shape[2]
    copies = []
    for i in range(4):
        start = pl.multiple_of((2 * (i % 2) + (x0 ^ (i // 2))) * wide, wide)
        copies.append(pltpu.make_async_copy(in_ref.at[:, pl.ds(start, wide)], chunks.at[i], sems.at[i]))
        copies[-1].start()
    n = 4 * LANES
    source = lax.broadcasted_iota(jnp.int32, (n, n), 0)
    goal = lax.broadcasted_iota(jnp.int32, (n, n), 1)
    q, z1, z2, row = goal // 128, goal // 64 % 2, goal // 32 % 2, goal % 32
    wanted = (z2 * 2 + z1) * 128 + (((q % 2) ^ z0) * 2 + ((q // 2) ^ c)) * 32 + row
    move = jnp.where(source == wanted, 1.0, 0.0).astype(my_ref.dtype)
    for i in range(4):
        copies[i].wait()
        for y in range(4):
            turned = jnp.dot(chunks[i, :, y * n : (y + 1) * n], move, preferred_element_type=jnp.float32)
            turned = turned.astype(my_ref.dtype)
            where = (y0 ^ (y % 2)) * 4 + (y // 2) * 2
            for rz in range(2):
                my_ref[i, where + rz] = turned[:, rz * LANES : (rz + 1) * LANES]
                other_ref[i, where + rz] = turned[:, (2 + rz) * LANES : (3 + rz) * LANES]


def sort_columns(at, tokens, limit):
    t, d = tokens.shape
    space = pl.BlockSpec(memory_space=pltpu.VMEM)
    return pl.pallas_call(
        sort_kernel,
        in_specs=[pl.BlockSpec(memory_space=pltpu.SMEM), pl.BlockSpec(memory_space=pl.ANY)],
        out_specs=[space, space],
        out_shape=[jax.ShapeDtypeStruct((4, 8, t, LANES), tokens.dtype)] * 2,
        scratch_shapes=[pltpu.VMEM((4, t, d // 4), tokens.dtype), pltpu.SemaphoreType.DMA((4,))],
        compiler_params=pltpu.CompilerParams(vmem_limit_bytes=limit),
        cost_estimate=pl.CostEstimate(flops=8 * LANES * t * d, bytes_accessed=4 * t * d, transcendentals=0),
        name="sort_columns",
    )(at, tokens)


def gradient_kernel(parts, mine_ref, theirs_ref, my_cot_ref, their_cot_ref, *out_refs):
    cot = jnp.concatenate([my_cot_ref[...].T, their_cot_ref[...].T], axis=1)
    starts = [sum(parts[:p]) for p in range(3)]
    for rx in range(2):
        for x1 in range(2):
            for ry in range(2):
                blocks = [
                    jnp.concatenate([mine_ref[rx * 2 + x1, ry * 4 + i], theirs_ref[rx * 2 + x1, ry * 4 + i]], axis=0)
                    for i in range(4)
                ]
                total = jnp.dot(cot, jnp.concatenate(blocks, axis=1), preferred_element_type=jnp.float32)
                total = total.astype(jnp.bfloat16)
                for y1 in range(2):
                    for rz in range(2):
                        i = y1 * 2 + rz
                        for p in range(3):
                            half, at = place_in(p, (rx, ry, rz), x1, y1)
                            out_refs[2 * p + half][:, at * LANES : (at + 1) * LANES] = total[
                                starts[p] : starts[p] + parts[p], i * LANES : (i + 1) * LANES
                            ]


def vmem_call(kernel, outs, name, flops, *operands, scalars=()):
    size = sum(a.size * a.dtype.itemsize for a in operands) + sum(o.size * o.dtype.itemsize for o in outs)
    space = pl.BlockSpec(memory_space=pltpu.VMEM)
    return pl.pallas_call(
        kernel,
        in_specs=[pl.BlockSpec(memory_space=pltpu.SMEM)] * len(scalars) + [space] * len(operands),
        out_specs=[space] * len(outs),
        out_shape=outs,
        compiler_params=pltpu.CompilerParams(vmem_limit_bytes=VMEM_LIMIT),
        cost_estimate=pl.CostEstimate(flops=flops, bytes_accessed=size, transcendentals=0),
        name=name,
    )(*scalars, *operands)


def rows_kernel(*refs):
    kept, came, out_ref = refs[0:6:2], refs[1:6:2], refs[6]
    sums = [k[...].astype(jnp.float32) + r[...].astype(jnp.float32) for k, r in zip(kept, came)]
    out_ref[...] = jnp.concatenate(sums, axis=0).T.astype(out_ref.dtype)


def columns_kernel(parts, in_ref, *out_refs):
    turned = in_ref[...].astype(jnp.float32).T.astype(in_ref.dtype)
    for p, out in enumerate(out_refs):
        start = sum(parts[:p])
        out[...] = turned[start : start + parts[p]]


def half_product(part, half, token_refs, weight_ref):
    tokens = [None] * 16
    for rx in range(2):
        for ry in range(2):
            for rz in range(2):
                for x1 in range(2):
                    for y1 in range(2):
                        side, at = place_in(part, (rx, ry, rz), x1, y1)
                        if side == half:
                            block = [ref[rx * 2 + x1, ry * 4 + y1 * 2 + rz] for ref in token_refs]
                            tokens[at] = jnp.concatenate(block, axis=0)
    return lax.dot_general(
        jnp.concatenate(tokens, axis=1), weight_ref[...], (((1,), (1,)), ((), ())), preferred_element_type=jnp.float32
    )


def forward_own_kernel(mine_ref, theirs_ref, *refs):
    for p in range(3):
        refs[3 + p][...] = half_product(p, 0, (mine_ref, theirs_ref), refs[p])
    refs[6][...] = theirs_ref[...]


def forward_kernel(first, tokens_ref, *refs):
    t = tokens_ref.shape[2]
    weights, before, out_ref = refs[:3], refs[3:6], refs[6]
    total = [before[p][first : first + t] + half_product(p, 1, (tokens_ref,), weights[p]) for p in range(3)]
    out_ref[...] = jnp.concatenate(total, axis=1).astype(out_ref.dtype)


def split_kernel(at_ref, partial_ref, own_ref, other_ref):
    z2 = at_ref[4]
    own_ref[...] = partial_ref[:, z2].astype(jnp.float32).sum(axis=0)
    other_ref[...] = partial_ref[:, 1 - z2].astype(jnp.float32).sum(axis=0).astype(other_ref.dtype)


def update_kernel(scale, own_ref, came_ref, master_ref, one_ref, two_ref, new_master, new_one, new_two, weights):
    gradient = (own_ref[...] + came_ref[...].astype(jnp.float32)) * scale
    one = 0.9 * one_ref[...] + 0.1 * gradient
    two = 0.999 * two_ref[...] + 0.001 * gradient * gradient
    first = one / (1.0 - 0.9**10)
    second = two / (1.0 - 0.999**10)
    master = master_ref[...]
    master = master - 0.01 * (first / (jnp.sqrt(second) + 1e-08) + 0.1 * master)
    new_one[...] = one
    new_two[...] = two
    new_master[...] = master
    weights[...] = master.astype(weights.dtype)


def copies_kernel(at_ref, own_ref, came_ref, out_ref):
    z2 = at_ref[4]
    for i in range(out_ref.shape[0]):
        out_ref[i, z2] = own_ref[...]
        out_ref[i, 1 - z2] = came_ref[...]


def halved(value):
    n = value.shape[1] // 2
    return value[:, :n], value[:, n:]


def on_device(tokens, cotangent, next_tokens, master, moment_one, moment_two):
    rows, f = master.shape
    t, d = tokens.shape
    half = d // 2
    parts = part_rows(f)
    me = lax.axis_index("grp") * 32 + lax.axis_index("intra")
    x, y, z, c = coordinates(me)
    at = jnp.stack([c, x % 2, y % 2, z % 2, z // 4]).astype(jnp.int32)
    bf16 = lambda *shape: jax.ShapeDtypeStruct(shape, jnp.bfloat16)
    f32 = lambda *shape: jax.ShapeDtypeStruct(shape, jnp.float32)
    other_core = lambda v: permute(v, lambda d: d ^ 1)
    flops = 4 * t * half * f

    their_cot = other_core(cotangent)
    mine, sent = sort_columns(at, tokens, FIRST_LIMIT)
    theirs = other_core(sent)
    halves = vmem_call(
        functools.partial(gradient_kernel, parts),
        [bf16(p, half // 2) for p in parts for _ in range(2)],
        "gradient",
        flops,
        mine,
        theirs,
        cotangent,
        their_cot,
    )
    later, *halves = lax.optimization_barrier((at, *halves))
    next_mine, next_sent = sort_columns(later, next_tokens, VMEM_LIMIT)
    last = []
    for p in range(3):
        kept, sent = halves[2 * p : 2 * p + 2]
        for i, axis in enumerate(ORDER[p]):
            came = permute(sent.astype(jnp.bfloat16), lambda d: neighbour(d, axis))
            if p == 0 and i == 0:
                came, next_sent = lax.optimization_barrier((came, next_sent))
            if i < 2:
                kept, sent = halved(kept.astype(jnp.float32) + came.astype(jnp.float32))
        last += [kept, came]
    (partial,) = vmem_call(rows_kernel, [bf16(16 * rows, f)], "rows", 0, *last)
    partial = lax.all_to_all(partial.reshape(8, 2, rows, f), AXES, 0, 0, tiled=True, axis_index_groups=groups())
    own, other = vmem_call(split_kernel, [f32(rows, f), bf16(rows, f)], "split", 0, partial, scalars=[at])
    new_master, new_moment_one, new_moment_two, weights = vmem_call(
        functools.partial(update_kernel, 1.0 / (t * DEVICES)),
        [f32(rows, f)] * 3 + [bf16(rows, f)],
        "update",
        0,
        own,
        permute(other, twin),
        master,
        moment_one,
        moment_two,
    )
    (copies,) = vmem_call(
        copies_kernel, [bf16(8, 2, rows, f)], "copies", 0, weights, permute(weights, twin), scalars=[at]
    )

    next_theirs = other_core(next_sent)
    copies = lax.all_to_all(copies, AXES, 0, 0, tiled=True, axis_index_groups=groups())
    held = vmem_call(
        functools.partial(columns_kernel, parts),
        [bf16(p, 16 * rows) for p in parts],
        "columns",
        0,
        copies.reshape(16 * rows, f),
    )
    owns, cames = [], []
    for p in range(3):
        own = held[p]
        for i, axis in enumerate(ORDER[p][::-1]):
            came = permute(own, lambda d: neighbour(d, axis))
            if i < 2:
                own = jnp.concatenate([own, came], axis=1)
        owns.append(own)
        cames.append(came)
    *before, next_theirs = vmem_call(
        forward_own_kernel,
        [f32(2 * t, p) for p in parts] + [bf16(*next_theirs.shape)],
        "forward_own",
        flops // 2,
        next_mine,
        next_theirs,
        *owns,
    )
    (their_out,) = vmem_call(
        functools.partial(forward_kernel, t), [bf16(t, f)], "forward_theirs", flops // 4, next_theirs, *cames, *before
    )
    their_out = other_core(their_out)
    (my_out,) = vmem_call(
        functools.partial(forward_kernel, 0), [f32(t, f)], "forward_mine", flops // 4, next_mine, *cames, *before
    )
    result = my_out + their_out.astype(jnp.float32)
    return (new_master, new_moment_one, new_moment_two, result.astype(jnp.bfloat16))


def solution(mesh):
    spec = P(AXES, None)
    return jax.shard_map(on_device, mesh=mesh, in_specs=(spec,) * 6, out_specs=(spec,) * 4, check_vma=False)
```

```python
import functools

import jax
import jax.numpy as jnp
from jax import lax
from jax.experimental import pallas as pl
from jax.experimental.pallas import tpu as pltpu
from jax.sharding import PartitionSpec as P

AXES = ("grp", "intra")
DEVICES = 256
SIZES = (4, 4, 8)
ORDER = ((0, 1, 2), (1, 2, 0), (2, 0, 1))
LANES = 128
VMEM_LIMIT = 24 * 1024 * 1024
FIRST_LIMIT = 48 * 1024 * 1024


def coordinates(d):
    return d // 64, d // 16 % 4, d // 2 % 8, d % 2


def flat(x, y, z, c):
    return x * 64 + y * 16 + z * 2 + c


def neighbour(d, axis):
    at, c = list(coordinates(d)[:3]), d % 2
    at[axis] = (at[axis] + (1 if at[axis] % 2 == c else -1)) % SIZES[axis]
    return flat(*at, c)


def permute(value, target):
    return lax.ppermute(value, AXES, [(d, target(d)) for d in range(DEVICES)])


def groups():
    seen = {}
    for d in range(DEVICES):
        x, y, z, c = coordinates(d)
        seen.setdefault((x % 2, y % 2, z % 2, c), []).append(d)
    return list(seen.values())


def part_rows(f):
    tiles = f // 16
    first = (tiles + 2) // 3 * 16
    return (first, first, f - 2 * first)


def place_in(part, rel, x1, y1):
    a, b, c = (rel[axis] for axis in ORDER[part])
    return a, (b * 2 + c) * 4 + x1 * 2 + y1


def sort_kernel(at_ref, in_ref, my_ref, other_ref, chunks, sems):
    c, x0, y0, z0 = (at_ref[i] for i in range(4))
    wide = chunks.shape[2]
    copies = []
    for i in range(4):
        start = pl.multiple_of((2 * (i % 2) + (x0 ^ (i // 2))) * wide, wide)
        copies.append(pltpu.make_async_copy(in_ref.at[:, pl.ds(start, wide)], chunks.at[i], sems.at[i]))
        copies[-1].start()
    n = 4 * LANES
    source = lax.broadcasted_iota(jnp.int32, (n, n), 0)
    goal = lax.broadcasted_iota(jnp.int32, (n, n), 1)
    q, r, row = goal // 128, goal // 32 % 4, goal % 32
    wanted = r * 128 + (((q % 2) ^ z0) * 2 + ((q // 2) ^ c)) * 32 + row
    move = jnp.where(source == wanted, 1.0, 0.0).astype(my_ref.dtype)
    for i in range(4):
        copies[i].wait()
        for y in range(4):
            turned = jnp.dot(chunks[i, :, y * n : (y + 1) * n], move, preferred_element_type=jnp.float32)
            turned = turned.astype(my_ref.dtype)
            where = (y0 ^ (y % 2)) * 4 + (y // 2) * 2
            for rz in range(2):
                my_ref[i, where + rz] = turned[:, rz * LANES : (rz + 1) * LANES]
                other_ref[i, where + rz] = turned[:, (2 + rz) * LANES : (3 + rz) * LANES]


def sort_columns(at, tokens, limit):
    t, d = tokens.shape
    space = pl.BlockSpec(memory_space=pltpu.VMEM)
    return pl.pallas_call(
        sort_kernel,
        in_specs=[pl.BlockSpec(memory_space=pltpu.SMEM), pl.BlockSpec(memory_space=pl.ANY)],
        out_specs=[space, space],
        out_shape=[jax.ShapeDtypeStruct((4, 8, t, LANES), tokens.dtype)] * 2,
        scratch_shapes=[pltpu.VMEM((4, t, d // 4), tokens.dtype), pltpu.SemaphoreType.DMA((4,))],
        compiler_params=pltpu.CompilerParams(vmem_limit_bytes=limit),
        cost_estimate=pl.CostEstimate(flops=8 * LANES * t * d, bytes_accessed=4 * t * d, transcendentals=0),
        name="sort_columns",
    )(at, tokens)


def gradient_kernel(parts, mine_ref, theirs_ref, my_cot_ref, their_cot_ref, *out_refs):
    cot = jnp.concatenate([my_cot_ref[...].T, their_cot_ref[...].T], axis=1)
    starts = [sum(parts[:p]) for p in range(3)]
    for rx in range(2):
        for x1 in range(2):
            for ry in range(2):
                blocks = [
                    jnp.concatenate([mine_ref[rx * 2 + x1, ry * 4 + i], theirs_ref[rx * 2 + x1, ry * 4 + i]], axis=0)
                    for i in range(4)
                ]
                total = jnp.dot(cot, jnp.concatenate(blocks, axis=1), preferred_element_type=jnp.float32)
                total = total.astype(jnp.bfloat16)
                for y1 in range(2):
                    for rz in range(2):
                        i = y1 * 2 + rz
                        for p in range(3):
                            half, at = place_in(p, (rx, ry, rz), x1, y1)
                            out_refs[2 * p + half][:, at * LANES : (at + 1) * LANES] = total[
                                starts[p] : starts[p] + parts[p], i * LANES : (i + 1) * LANES
                            ]


def vmem_call(kernel, outs, name, flops, *operands):
    size = sum(a.size * a.dtype.itemsize for a in operands) + sum(o.size * o.dtype.itemsize for o in outs)
    space = pl.BlockSpec(memory_space=pltpu.VMEM)
    return pl.pallas_call(
        kernel,
        in_specs=[space] * len(operands),
        out_specs=[space] * len(outs),
        out_shape=outs,
        compiler_params=pltpu.CompilerParams(vmem_limit_bytes=VMEM_LIMIT),
        cost_estimate=pl.CostEstimate(flops=flops, bytes_accessed=size, transcendentals=0),
        name=name,
    )(*operands)


def rows_kernel(*refs):
    kept, came, out_ref = refs[0:6:2], refs[1:6:2], refs[6]
    sums = [k[...].astype(jnp.float32) + r[...].astype(jnp.float32) for k, r in zip(kept, came)]
    out_ref[...] = jnp.concatenate(sums, axis=0).T.astype(out_ref.dtype)


def columns_kernel(parts, in_ref, *out_refs):
    turned = in_ref[...].astype(jnp.float32).T.astype(in_ref.dtype)
    for p, out in enumerate(out_refs):
        start = sum(parts[:p])
        out[...] = turned[start : start + parts[p]]


def half_product(part, half, token_refs, weight_ref):
    tokens = [None] * 16
    for rx in range(2):
        for ry in range(2):
            for rz in range(2):
                for x1 in range(2):
                    for y1 in range(2):
                        side, at = place_in(part, (rx, ry, rz), x1, y1)
                        if side == half:
                            block = [ref[rx * 2 + x1, ry * 4 + y1 * 2 + rz] for ref in token_refs]
                            tokens[at] = jnp.concatenate(block, axis=0)
    return lax.dot_general(
        jnp.concatenate(tokens, axis=1), weight_ref[...], (((1,), (1,)), ((), ())), preferred_element_type=jnp.float32
    )


def forward_own_kernel(mine_ref, theirs_ref, *refs):
    for p in range(3):
        refs[3 + p][...] = half_product(p, 0, (mine_ref, theirs_ref), refs[p])
    refs[6][...] = theirs_ref[...]


def forward_kernel(first, tokens_ref, *refs):
    t = tokens_ref.shape[2]
    weights, before, out_ref = refs[:3], refs[3:6], refs[6]
    total = [before[p][first : first + t] + half_product(p, 1, (tokens_ref,), weights[p]) for p in range(3)]
    out_ref[...] = jnp.concatenate(total, axis=1).astype(out_ref.dtype)


def update_kernel(scale, partial_ref, master_ref, one_ref, two_ref, new_master, new_one, new_two, copies):
    gradient = partial_ref[...].astype(jnp.float32).sum(axis=0) * scale
    one = 0.9 * one_ref[...] + 0.1 * gradient
    two = 0.999 * two_ref[...] + 0.001 * gradient * gradient
    first = one / (1.0 - 0.9**10)
    second = two / (1.0 - 0.999**10)
    master = master_ref[...]
    master = master - 0.01 * (first / (jnp.sqrt(second) + 1e-08) + 0.1 * master)
    new_one[...] = one
    new_two[...] = two
    new_master[...] = master
    copies[...] = jnp.broadcast_to(master.astype(copies.dtype)[None], copies.shape)


def halved(value):
    n = value.shape[1] // 2
    return value[:, :n], value[:, n:]


def on_device(tokens, cotangent, next_tokens, master, moment_one, moment_two):
    rows, f = master.shape
    t, d = tokens.shape
    half = d // 2
    parts = part_rows(f)
    me = lax.axis_index("grp") * 32 + lax.axis_index("intra")
    x, y, z, c = coordinates(me)
    at = jnp.stack([c, x % 2, y % 2, z % 2]).astype(jnp.int32)
    bf16 = lambda *shape: jax.ShapeDtypeStruct(shape, jnp.bfloat16)
    f32 = lambda *shape: jax.ShapeDtypeStruct(shape, jnp.float32)
    other_core = lambda v: permute(v, lambda d: d ^ 1)
    flops = 4 * t * half * f

    their_cot = other_core(cotangent)
    mine, sent = sort_columns(at, tokens, FIRST_LIMIT)
    theirs = other_core(sent)
    halves = vmem_call(
        functools.partial(gradient_kernel, parts),
        [bf16(p, half // 2) for p in parts for _ in range(2)],
        "gradient",
        flops,
        mine,
        theirs,
        cotangent,
        their_cot,
    )
    later, *halves = lax.optimization_barrier((at, *halves))
    next_mine, next_sent = sort_columns(later, next_tokens, VMEM_LIMIT)
    last = []
    for p in range(3):
        kept, sent = halves[2 * p : 2 * p + 2]
        for i, axis in enumerate(ORDER[p]):
            came = permute(sent.astype(jnp.bfloat16), lambda d: neighbour(d, axis))
            if p == 0 and i == 0:
                came, next_sent = lax.optimization_barrier((came, next_sent))
            if i < 2:
                kept, sent = halved(kept.astype(jnp.float32) + came.astype(jnp.float32))
        last += [kept, came]
    (partial,) = vmem_call(rows_kernel, [bf16(16 * rows, f)], "rows", 0, *last)
    partial = partial.reshape(16, rows, f)
    partial = lax.all_to_all(partial, AXES, 0, 0, tiled=True, axis_index_groups=groups())
    new_master, new_moment_one, new_moment_two, copies = vmem_call(
        functools.partial(update_kernel, 1.0 / (t * DEVICES)),
        [f32(rows, f)] * 3 + [bf16(16, rows, f)],
        "update",
        0,
        partial,
        master,
        moment_one,
        moment_two,
    )

    next_theirs = other_core(next_sent)
    copies = lax.all_to_all(copies, AXES, 0, 0, tiled=True, axis_index_groups=groups())
    held = vmem_call(
        functools.partial(columns_kernel, parts),
        [bf16(p, 16 * rows) for p in parts],
        "columns",
        0,
        copies.reshape(16 * rows, f),
    )
    owns, cames = [], []
    for p in range(3):
        own = held[p]
        for i, axis in enumerate(ORDER[p][::-1]):
            came = permute(own, lambda d: neighbour(d, axis))
            if i < 2:
                own = jnp.concatenate([own, came], axis=1)
        owns.append(own)
        cames.append(came)
    *before, next_theirs = vmem_call(
        forward_own_kernel,
        [f32(2 * t, p) for p in parts] + [bf16(*next_theirs.shape)],
        "forward_own",
        flops // 2,
        next_mine,
        next_theirs,
        *owns,
    )
    (their_out,) = vmem_call(
        functools.partial(forward_kernel, t), [bf16(t, f)], "forward_theirs", flops // 4, next_theirs, *cames, *before
    )
    their_out = other_core(their_out)
    (my_out,) = vmem_call(
        functools.partial(forward_kernel, 0), [f32(t, f)], "forward_mine", flops // 4, next_mine, *cames, *before
    )
    result = my_out + their_out.astype(jnp.float32)
    return (new_master, new_moment_one, new_moment_two, result.astype(jnp.bfloat16))


def solution(mesh):
    spec = P(AXES, None)
    return jax.shard_map(on_device, mesh=mesh, in_specs=(spec,) * 6, out_specs=(spec,) * 4, check_vma=False)
```

```python
import functools

import jax
import jax.numpy as jnp
from jax import lax
from jax.experimental import pallas as pl
from jax.experimental.pallas import tpu as pltpu
from jax.sharding import PartitionSpec as P

AXES = ("grp", "intra")
DEVICES = 256
SIZES = (4, 4, 8)
ORDER = ((0, 1, 2), (1, 2, 0), (2, 0, 1))
LANES = 128
VMEM_LIMIT = 24 * 1024 * 1024
FIRST_LIMIT = 48 * 1024 * 1024


def coordinates(d):
    return d // 64, d // 16 % 4, d // 2 % 8, d % 2


def flat(x, y, z, c):
    return x * 64 + y * 16 + z * 2 + c


def neighbour(d, axis):
    at, c = list(coordinates(d)[:3]), d % 2
    at[axis] = (at[axis] + (1 if at[axis] % 2 == c else -1)) % SIZES[axis]
    return flat(*at, c)


def permute(value, target):
    return lax.ppermute(value, AXES, [(d, target(d)) for d in range(DEVICES)])


def side(v, c):
    return (v // 2) ^ (v % 2 * (1 - c))


def rest(v, c):
    return v // 2 * (1 - c) + v % 2 * c


def groups():
    seen = {}
    for d in range(DEVICES):
        x, y, z, c = coordinates(d)
        seen.setdefault((side(x, c), side(y, c), z % 2, c), []).append(d)
    return list(seen.values())


def part_rows(f):
    tiles = f // 16
    first = (tiles + 2) // 3 * 16
    return (first, first, f - 2 * first)


def place_in(part, rel, x1, y1):
    a, b, c = (rel[axis] for axis in ORDER[part])
    return a, (b * 2 + c) * 4 + x1 * 2 + y1


def sort_kernel(at_ref, in_ref, my_ref, other_ref, chunks, sems):
    c, x0, y0, z0 = (at_ref[i] for i in range(4))
    wide = chunks.shape[2]
    copies, theirs = [], []
    for i in range(4):
        near, far = x0 ^ (i // 2), i % 2
        x = jnp.where(c == 0, 2 * far + (near ^ far), 2 * near + far)
        theirs.append((at_ref[4] ^ side(x, 1 - c)) * 2 + rest(x, 1 - c))
        start = pl.multiple_of(x * wide, wide)
        copies.append(pltpu.make_async_copy(in_ref.at[:, pl.ds(start, wide)], chunks.at[i], sems.at[i]))
        copies[-1].start()
    n = 4 * LANES
    source = lax.broadcasted_iota(jnp.int32, (n, n), 0)
    goal = lax.broadcasted_iota(jnp.int32, (n, n), 1)
    q, r, row = goal // 128, goal // 32 % 4, goal % 32
    wanted = r * 128 + (((q % 2) ^ z0) * 2 + ((q // 2) ^ c)) * 32 + row
    move = jnp.where(source == wanted, 1.0, 0.0).astype(my_ref.dtype)
    for i in range(4):
        copies[i].wait()
        for y in range(4):
            turned = jnp.dot(chunks[i, :, y * n : (y + 1) * n], move, preferred_element_type=jnp.float32)
            turned = turned.astype(my_ref.dtype)
            where = (y0 ^ side(y, c)) * 4 + rest(y, c) * 2
            there = (at_ref[5] ^ side(y, 1 - c)) * 4 + rest(y, 1 - c) * 2
            for rz in range(2):
                my_ref[i, where + rz] = turned[:, rz * LANES : (rz + 1) * LANES]
                other_ref[theirs[i], there + rz] = turned[:, (2 + rz) * LANES : (3 + rz) * LANES]


def sort_columns(at, tokens, limit):
    t, d = tokens.shape
    space = pl.BlockSpec(memory_space=pltpu.VMEM)
    return pl.pallas_call(
        sort_kernel,
        in_specs=[pl.BlockSpec(memory_space=pltpu.SMEM), pl.BlockSpec(memory_space=pl.ANY)],
        out_specs=[space, space],
        out_shape=[jax.ShapeDtypeStruct((4, 8, t, LANES), tokens.dtype)] * 2,
        scratch_shapes=[pltpu.VMEM((4, t, d // 4), tokens.dtype), pltpu.SemaphoreType.DMA((4,))],
        compiler_params=pltpu.CompilerParams(vmem_limit_bytes=limit),
        cost_estimate=pl.CostEstimate(flops=8 * LANES * t * d, bytes_accessed=4 * t * d, transcendentals=0),
        name="sort_columns",
    )(at, tokens)


def gradient_kernel(parts, mine_ref, theirs_ref, my_cot_ref, their_cot_ref, *out_refs):
    cot = jnp.concatenate([my_cot_ref[...].T, their_cot_ref[...].T], axis=1)
    starts = [sum(parts[:p]) for p in range(3)]
    for rx in range(2):
        for x1 in range(2):
            for ry in range(2):
                blocks = [
                    jnp.concatenate([mine_ref[rx * 2 + x1, ry * 4 + i], theirs_ref[rx * 2 + x1, ry * 4 + i]], axis=0)
                    for i in range(4)
                ]
                total = jnp.dot(cot, jnp.concatenate(blocks, axis=1), preferred_element_type=jnp.float32)
                total = total.astype(jnp.bfloat16)
                for y1 in range(2):
                    for rz in range(2):
                        i = y1 * 2 + rz
                        for p in range(3):
                            half, at = place_in(p, (rx, ry, rz), x1, y1)
                            out_refs[2 * p + half][:, at * LANES : (at + 1) * LANES] = total[
                                starts[p] : starts[p] + parts[p], i * LANES : (i + 1) * LANES
                            ]


def vmem_call(kernel, outs, name, flops, *operands):
    size = sum(a.size * a.dtype.itemsize for a in operands) + sum(o.size * o.dtype.itemsize for o in outs)
    space = pl.BlockSpec(memory_space=pltpu.VMEM)
    return pl.pallas_call(
        kernel,
        in_specs=[space] * len(operands),
        out_specs=[space] * len(outs),
        out_shape=outs,
        compiler_params=pltpu.CompilerParams(vmem_limit_bytes=VMEM_LIMIT),
        cost_estimate=pl.CostEstimate(flops=flops, bytes_accessed=size, transcendentals=0),
        name=name,
    )(*operands)


def rows_kernel(*refs):
    kept, came, out_ref = refs[0:6:2], refs[1:6:2], refs[6]
    sums = [k[...].astype(jnp.float32) + r[...].astype(jnp.float32) for k, r in zip(kept, came)]
    out_ref[...] = jnp.concatenate(sums, axis=0).T.astype(out_ref.dtype)


def columns_kernel(parts, in_ref, *out_refs):
    turned = in_ref[...].astype(jnp.float32).T.astype(in_ref.dtype)
    for p, out in enumerate(out_refs):
        start = sum(parts[:p])
        out[...] = turned[start : start + parts[p]]


def half_product(part, half, token_refs, weight_ref):
    tokens = [None] * 16
    for rx in range(2):
        for ry in range(2):
            for rz in range(2):
                for x1 in range(2):
                    for y1 in range(2):
                        side, at = place_in(part, (rx, ry, rz), x1, y1)
                        if side == half:
                            block = [ref[rx * 2 + x1, ry * 4 + y1 * 2 + rz] for ref in token_refs]
                            tokens[at] = jnp.concatenate(block, axis=0)
    return lax.dot_general(
        jnp.concatenate(tokens, axis=1), weight_ref[...], (((1,), (1,)), ((), ())), preferred_element_type=jnp.float32
    )


def forward_own_kernel(mine_ref, theirs_ref, *refs):
    for p in range(3):
        refs[3 + p][...] = half_product(p, 0, (mine_ref, theirs_ref), refs[p])
    refs[6][...] = theirs_ref[...]


def forward_kernel(first, tokens_ref, *refs):
    t = tokens_ref.shape[2]
    weights, before, out_ref = refs[:3], refs[3:6], refs[6]
    total = [before[p][first : first + t] + half_product(p, 1, (tokens_ref,), weights[p]) for p in range(3)]
    out_ref[...] = jnp.concatenate(total, axis=1).astype(out_ref.dtype)


def update_kernel(scale, partial_ref, master_ref, one_ref, two_ref, new_master, new_one, new_two, copies):
    gradient = partial_ref[...].astype(jnp.float32).sum(axis=0) * scale
    one = 0.9 * one_ref[...] + 0.1 * gradient
    two = 0.999 * two_ref[...] + 0.001 * gradient * gradient
    first = one / (1.0 - 0.9**10)
    second = two / (1.0 - 0.999**10)
    master = master_ref[...]
    master = master - 0.01 * (first / (jnp.sqrt(second) + 1e-08) + 0.1 * master)
    new_one[...] = one
    new_two[...] = two
    new_master[...] = master
    copies[...] = jnp.broadcast_to(master.astype(copies.dtype)[None], copies.shape)


def halved(value):
    n = value.shape[1] // 2
    return value[:, :n], value[:, n:]


def on_device(tokens, cotangent, next_tokens, master, moment_one, moment_two):
    rows, f = master.shape
    t, d = tokens.shape
    half = d // 2
    parts = part_rows(f)
    me = lax.axis_index("grp") * 32 + lax.axis_index("intra")
    x, y, z, c = coordinates(me)
    at = jnp.stack([c, side(x, c), side(y, c), z % 2, side(x, 1 - c), side(y, 1 - c)]).astype(jnp.int32)
    bf16 = lambda *shape: jax.ShapeDtypeStruct(shape, jnp.bfloat16)
    f32 = lambda *shape: jax.ShapeDtypeStruct(shape, jnp.float32)
    other_core = lambda v: permute(v, lambda d: d ^ 1)
    flops = 4 * t * half * f

    their_cot = other_core(cotangent)
    mine, sent = sort_columns(at, tokens, FIRST_LIMIT)
    theirs = other_core(sent)
    halves = vmem_call(
        functools.partial(gradient_kernel, parts),
        [bf16(p, half // 2) for p in parts for _ in range(2)],
        "gradient",
        flops,
        mine,
        theirs,
        cotangent,
        their_cot,
    )
    later, *halves = lax.optimization_barrier((at, *halves))
    next_mine, next_sent = sort_columns(later, next_tokens, VMEM_LIMIT)
    last = []
    for p in range(3):
        kept, sent = halves[2 * p : 2 * p + 2]
        for i, axis in enumerate(ORDER[p]):
            came = permute(sent.astype(jnp.bfloat16), lambda d: neighbour(d, axis))
            if p == 0 and i == 0:
                came, next_sent = lax.optimization_barrier((came, next_sent))
            if i < 2:
                kept, sent = halved(kept.astype(jnp.float32) + came.astype(jnp.float32))
        last += [kept, came]
    (partial,) = vmem_call(rows_kernel, [bf16(16 * rows, f)], "rows", 0, *last)
    partial = partial.reshape(16, rows, f)
    partial = lax.all_to_all(partial, AXES, 0, 0, tiled=True, axis_index_groups=groups())
    new_master, new_moment_one, new_moment_two, copies = vmem_call(
        functools.partial(update_kernel, 1.0 / (t * DEVICES)),
        [f32(rows, f)] * 3 + [bf16(16, rows, f)],
        "update",
        0,
        partial,
        master,
        moment_one,
        moment_two,
    )

    next_theirs = other_core(next_sent)
    copies = lax.all_to_all(copies, AXES, 0, 0, tiled=True, axis_index_groups=groups())
    held = vmem_call(
        functools.partial(columns_kernel, parts),
        [bf16(p, 16 * rows) for p in parts],
        "columns",
        0,
        copies.reshape(16 * rows, f),
    )
    owns, cames = [], []
    for p in range(3):
        own = held[p]
        for i, axis in enumerate(ORDER[p][::-1]):
            came = permute(own, lambda d: neighbour(d, axis))
            if i < 2:
                own = jnp.concatenate([own, came], axis=1)
        owns.append(own)
        cames.append(came)
    *before, next_theirs = vmem_call(
        forward_own_kernel,
        [f32(2 * t, p) for p in parts] + [bf16(*next_theirs.shape)],
        "forward_own",
        flops // 2,
        next_mine,
        next_theirs,
        *owns,
    )
    (their_out,) = vmem_call(
        functools.partial(forward_kernel, t), [bf16(t, f)], "forward_theirs", flops // 4, next_theirs, *cames, *before
    )
    their_out = other_core(their_out)
    (my_out,) = vmem_call(
        functools.partial(forward_kernel, 0), [f32(t, f)], "forward_mine", flops // 4, next_mine, *cames, *before
    )
    result = my_out + their_out.astype(jnp.float32)
    return (new_master, new_moment_one, new_moment_two, result.astype(jnp.bfloat16))


def solution(mesh):
    spec = P(AXES, None)
    return jax.shard_map(on_device, mesh=mesh, in_specs=(spec,) * 6, out_specs=(spec,) * 4, check_vma=False)
```
